512 devices in a mesh: row: 32 (over y, x), col: 16 (over z, core).
Axes of the slice: x: 4, y: 8, z: 8, core: 2. Of those that a mesh axis runs over, the one named last changes fastest.
Arguments:
- resident_inverse: bfloat16 [24576, 24576], P('row', 'col')
- factor: bfloat16 [3, 24576, 512], P(None, 'row', 'col'), may hold values from -0.4375 to 0.4375
- diag_inverse: float32 [3, 512, 512], P(None, None, 'col'), may hold values from -4 to 4
- anc_tiles: int32 [3, 64], replicated, may hold values from -1 to 95, as said below
- slot_tile: int32 [96], replicated, may hold values from 0 to 95, as said below
Outputs:
- new_cols: bfloat16 [3, 24576, 512], P(None, 'row', 'col')
- diag_blocks: float32 [3, 512, 512], P(None, None, 'col')
The draws below stay inside these ranges and needn't reach their ends.
Inputs may be any that keep to these rules, and one draw needn't show every extreme that they name: `anc_tiles`: row j lists the ancestor tiles of supernode j in ascending order, each at most once, followed by -1 in unused entries; every list holds tile 96 - 1; list 0 is full and list 2 has fewer than 32 tiles. A permutation of the tiles; slot s holds tile slot_tile[s], and each tile is stored within the same block of 6 consecutive slots as its own index. `resident_inverse` is symmetric.
All inputs are finite; a program needn't handle non-finite values.
Results may differ from the reference program's by a relative error of at most 0.017.
Values may be sent and summed in bfloat16 or wider, within the bound.
No kernel may reach another device: no remote copies, remote signals or barrier semaphores. Data moves between devices by JAX's collectives and lax.ppermute only.
A program may use at most 64 MiB of HBM per device.

```python
import jax
import jax.numpy as jnp
from jax import lax

NA = 24576
W = 512
TB = 256
SUPERS = 3
MAXT = 64
NT = 96
OWN_TILES = 6
N_ROW = 32
N_COL = 16


def draw_resident_inverse(key, part):
    key_main = jax.random.fold_in(key, 101)
    spread = 1.5 / NA ** 0.5
    noise = jax.random.normal(key_main, (NA, NA), jnp.float32)
    sym = (noise + noise.T) * (0.70710678 * spread)
    sym = sym + jnp.eye(NA, dtype=jnp.float32)
    return sym.astype(jnp.bfloat16)


def draw_anc_tiles(key, part):
    tile_ids = jnp.arange(NT, dtype=jnp.int32)
    key_pick = jax.random.fold_in(key, 303)
    count_one = jax.random.randint(jax.random.fold_in(key, 404), (), MAXT // 2, MAXT)
    count_two = jax.random.randint(jax.random.fold_in(key, 505), (), MAXT // 4, MAXT // 2)
    counts = jnp.stack([jnp.int32(MAXT), count_one.astype(jnp.int32), count_two.astype(jnp.int32)])
    listing = []
    for which in range(SUPERS):
        raw_scores = jax.random.randint(jax.random.fold_in(key_pick, which), (NT,), 0, NT)
        scores = (raw_scores + tile_ids) * NT + tile_ids
        scores = jnp.where(tile_ids == NT - 1, 4 * NT * NT, scores)
        ranking = jnp.argsort(-scores, stable=True).astype(jnp.int32)
        chosen = ranking[:MAXT]
        in_list = jnp.arange(MAXT, dtype=jnp.int32) < counts[which % 3]
        chosen = jnp.where(in_list, chosen, NT + 1)
        chosen = jnp.sort(chosen)
        listing.append(jnp.where(chosen > NT - 1, -1, chosen).astype(jnp.int32))
    return jnp.stack(listing)


def draw_slot_tile(key, part):
    tile_ids = jnp.arange(NT, dtype=jnp.int32)
    raw_scores = jax.random.randint(jax.random.fold_in(key, 606), (NT,), 0, NT)
    groups = tile_ids // OWN_TILES
    scores = groups * (NT * NT) + raw_scores * NT + tile_ids
    return jnp.argsort(scores, stable=True).astype(jnp.int32)


def strengthened(drawn, rng, source, target, blocks, factor):
    def block_of(position):
        return (jnp.arange(drawn.shape[position]) // (drawn.shape[position] // blocks)).reshape((-1,) + (1,) * (drawn.ndim - 1 - position))

    first = jax.random.permutation(rng, blocks)[block_of(target)]
    far = (block_of(target) + blocks // 2) % blocks
    return jnp.where((block_of(source) == first) | (block_of(source) == far), factor * drawn, drawn)


def steps_of(own_key, extent, pieces, smallest, largest):
    gain = 1.0
    for axis_at, parts in pieces:
        draws = jax.random.uniform(jax.random.fold_in(jax.random.fold_in(own_key, 6), axis_at), (parts,), jnp.float32, smallest / len(pieces), largest / len(pieces))
        gain = gain * jnp.repeat(jnp.exp(draws), extent[axis_at] // parts).reshape((-1,) + (1,) * (len(extent) - 1 - axis_at))
    return gain


def gaussian(key, extent, deviation, limit, shards=(), kind=jnp.bfloat16):
    drawn = deviation * jax.random.normal(key, extent, jnp.float32)
    if shards:
        drawn = drawn * steps_of(key, extent, shards, -0.22, 0.18)
    return jnp.clip(drawn, -limit, limit).astype(kind)


def bell_draw_with(own_key, dims, scale, most, split, heavy, held_as=jnp.bfloat16):
    array = scale * jax.random.normal(own_key, dims, jnp.float32)
    if split:
        array = array * steps_of(own_key, dims, split, -0.22, 0.18)
    return jnp.clip(strengthened(array, jax.random.fold_in(own_key, 3), *heavy), -most, most).astype(held_as)


def setup_inputs(seed: int = 0) -> dict:
    seeds = jax.random.split(jax.random.key(seed), 6)
    resident_inverse = draw_resident_inverse(jax.random.fold_in(seeds[5], 71), 0)
    factor = bell_draw_with(seeds[1], (SUPERS, NA, W), (NA // N_ROW) ** -0.5, 0.4375, ((1, 32), (2, 16)), (1, 2, 32, 2.75))
    diag_inverse = gaussian(seeds[2], (SUPERS, W, W), 0.5, 4.0, ((2, 16),), jnp.float32)
    anc_tiles = draw_anc_tiles(jax.random.fold_in(seeds[5], 71), 0)
    slot_tile = draw_slot_tile(jax.random.fold_in(seeds[5], 71), 0)
    return {"resident_inverse": resident_inverse, "factor": factor, "diag_inverse": diag_inverse, "anc_tiles": anc_tiles, "slot_tile": slot_tile}


def slot_rows(anc_tiles, slot_tile):
    tile_ids = jnp.arange(NT, dtype=jnp.int32)
    listed = jnp.sum((anc_tiles[:, :, None] == tile_ids[None, None, :]).astype(jnp.float32), axis=1)
    onehot = (slot_tile[:, None] == tile_ids[None, :]).astype(jnp.float32)
    slot_mask = jnp.dot(listed, onehot.T, precision=lax.Precision.HIGHEST)
    return jnp.repeat(slot_mask, TB, axis=1)


def reference(resident_inverse, factor, diag_inverse, anc_tiles, slot_tile):
    row_mask = slot_rows(anc_tiles, slot_tile)
    masked = factor * row_mask.astype(jnp.bfloat16)[:, :, None]
    col_width = NA // N_COL

    def add_block(running, column_block):
        offset = column_block * col_width
        columns = lax.dynamic_slice_in_dim(resident_inverse, offset, col_width, 1).astype(jnp.float32)
        picked = lax.dynamic_slice_in_dim(masked, offset, col_width, 1).astype(jnp.float32)
        partial_value = jnp.einsum("rk,skw->srw", columns, picked, precision=lax.Precision.HIGHEST)
        rounded = lax.optimization_barrier(partial_value.astype(jnp.bfloat16))
        return running + rounded.astype(jnp.float32), None

    summed, _ = lax.scan(add_block, jnp.zeros((SUPERS, NA, W), jnp.float32), jnp.arange(N_COL, dtype=jnp.int32))
    new_cols = (-(summed * row_mask[:, :, None])).astype(jnp.bfloat16)
    diag_blocks = diag_inverse + jnp.einsum("snw,snv->swv", masked.astype(jnp.float32), summed, precision=lax.Precision.HIGHEST)
    return new_cols, diag_blocks
```

```python
import jax
import jax.numpy as jnp
from jax import lax
from jax.experimental import pallas as pl
from jax.experimental.pallas import tpu as pltpu
from jax.sharding import Mesh, PartitionSpec as P

AXES = ("y", "x", "z", "k")
NY, NX, NZ, NK = 8, 4, 8, 2
SUPERS = 3
W = 512
WL = 32
ROWS = 768
SLOTS = 3
TB = 256


def linear(y, x, z, k):
    return ((y * NX + x) * NZ + z) * NK + k


def permutation(f):
    pairs = []
    for y in range(NY):
        for x in range(NX):
            for z in range(NZ):
                for k in range(NK):
                    pairs.append((linear(y, x, z, k), linear(*f(y, x, z, k))))
    return pairs


NT_DIMS = (((1,), (1,)), ((), ()))


def product_kernel(k_ref, g_ref, own_ref, sib_ref, m0_ref, m1_ref, m2_ref, part_ref, diag_ref, acc):
    step = pl.program_id(0)
    lhs = g_ref[...].reshape(NZ * SUPERS * WL, ROWS)

    @pl.when(step == 0)
    def _():
        acc[...] = lax.dot_general(lhs, own_ref[...], NT_DIMS, preferred_element_type=jnp.float32)

    @pl.when(step == 1)
    def _():
        acc[...] += lax.dot_general(lhs, own_ref[...], NT_DIMS, preferred_element_type=jnp.float32)

    @pl.when(step >= 2)
    def _():
        acc[...] += lax.dot_general(lhs, sib_ref[...], NT_DIMS, preferred_element_type=jnp.float32)

    @pl.when(step == 3)
    def _():
        part = acc[...].astype(jnp.bfloat16)
        part_ref[...] = part
        split = part.reshape(NZ, SUPERS, WL, ROWS)
        for j, m_ref in enumerate((m0_ref, m1_ref, m2_ref)):
            mine = split[:, j].reshape(NZ * WL, ROWS)
            diag = lax.dot_general(m_ref[...], mine, NT_DIMS, preferred_element_type=jnp.float32)
            diag_ref[:, j * NZ * WL:(j + 1) * NZ * WL] = diag.astype(jnp.bfloat16)


def products(core, gathered, own, sib, rows):
    n = NZ * SUPERS * WL

    def block_of(step, k_ref):
        side = jnp.where(step < 2, k_ref[0], 1 - k_ref[0])
        return 2 * side + step % 2

    whole = pl.BlockSpec((W, ROWS), lambda s, k: (0, 0))
    return pl.pallas_call(
        product_kernel,
        grid_spec=pltpu.PrefetchScalarGridSpec(
            num_scalar_prefetch=1,
            grid=(4,),
            in_specs=[
                pl.BlockSpec((NZ, 1, SUPERS * WL, ROWS), lambda s, k: (0, block_of(s, k), 0, 0)),
                pl.BlockSpec((ROWS, ROWS), lambda s, k: (0, jnp.minimum(s, 1))),
                pl.BlockSpec((ROWS, ROWS), lambda s, k: (0, jnp.maximum(s, 2) - 2)),
                whole, whole, whole,
            ],
            out_specs=[
                pl.BlockSpec((n, ROWS), lambda s, k: (0, 0)),
                pl.BlockSpec((W, n), lambda s, k: (0, 0)),
            ],
            scratch_shapes=[pltpu.VMEM((n, ROWS), jnp.float32)],
        ),
        out_shape=[
            jax.ShapeDtypeStruct((n, ROWS), jnp.bfloat16),
            jax.ShapeDtypeStruct((W, n), jnp.bfloat16),
        ],
        compiler_params=pltpu.CompilerParams(vmem_limit_bytes=44 * 1024 * 1024),
        cost_estimate=pl.CostEstimate(flops=4_900_000_000, bytes_accessed=14_000_000, transcendentals=0),
    )(core, gathered, own, sib, *rows)


def on_device(resident, factor, diag_inverse, anc_tiles, slot_tile):
    core = lax.axis_index("k")
    row = lax.axis_index("y") * NX + lax.axis_index("x")
    sib = lax.ppermute(resident, AXES, permutation(lambda y, x, z, k: (y, x, z, 1 - k)))

    slots = lax.dynamic_slice(slot_tile, (row * SLOTS,), (SLOTS,))
    listed = jnp.any(anc_tiles[:, None, :] == slots[None, :, None], axis=2)
    mask = jnp.repeat(listed, TB, axis=1)
    masked = jnp.where(mask[:, None, :], factor.transpose(0, 2, 1), jnp.bfloat16(0))
    flat = masked.reshape(SUPERS * WL, ROWS)

    moved = lax.ppermute(flat, AXES, permutation(lambda y, x, z, k: (z, x, y, k)))
    gathered = lax.all_gather(moved, ("y", "x"), axis=0, tiled=False)
    gathered = gathered.reshape(NZ, NX, SUPERS * WL, ROWS)
    rows = [lax.all_gather(masked[j], ("z", "k"), axis=0, tiled=True) for j in range(SUPERS)]

    part, diag = products(core.reshape(1), gathered, resident, sib, rows)

    summed = lax.psum_scatter(part, "z", scatter_dimension=0, tiled=True)
    summed = summed.reshape(SUPERS, WL, ROWS).astype(jnp.float32)
    new_cols = jnp.where(mask[:, None, :], -summed, 0.0).astype(jnp.bfloat16).transpose(0, 2, 1)

    spread = lax.all_to_all(diag.reshape(NY * NX, W // (NY * NX), SUPERS * NZ * WL), ("y", "x"), 0, 0, tiled=True)
    slab = jnp.sum(spread.astype(jnp.float32), axis=0).reshape(W // (NY * NX), SUPERS, NZ, WL)
    slab = slab.transpose(2, 0, 1, 3).reshape(NZ, W // (NY * NX), SUPERS * WL)
    slab = jnp.sum(lax.all_to_all(slab, "z", 0, 0, tiled=True), axis=0).astype(jnp.bfloat16)
    copies = jnp.broadcast_to(slab[None], (NY * NX,) + slab.shape)
    total = lax.all_to_all(copies, ("y", "x"), 0, 0, tiled=True)
    total = total.reshape(W, SUPERS, WL).transpose(1, 0, 2).astype(jnp.float32)
    return new_cols, diag_inverse + total


def solution(mesh):
    fine = Mesh(mesh.devices.reshape(NY, NX, NZ, NK), AXES)
    row, col = ("y", "x"), ("z", "k")
    return jax.shard_map(
        on_device,
        mesh=fine,
        in_specs=(P(row, col), P(None, row, col), P(None, None, col), P(), P()),
        out_specs=(P(None, row, col), P(None, None, col)),
        check_vma=False,
    )
```

```python
import jax
import jax.numpy as jnp
from jax import lax
from jax.experimental import pallas as pl
from jax.experimental.pallas import tpu as pltpu
from jax.sharding import Mesh, PartitionSpec as P

AXES = ("y", "x", "z", "k")
ROW, COL = ("y", "x"), ("z", "k")
NY, NX, NZ, NK = 8, 4, 8, 2
SUPERS = 3
W = 512
WL = 32
SL = SUPERS * WL
ROWS = 768
SLOTS = 3
TB = 256
NT_DIMS = (((1,), (1,)), ((), ()))


def linear(y, x, z, k):
    return ((y * NX + x) * NZ + z) * NK + k


def permutation(f):
    pairs = []
    for y in range(NY):
        for x in range(NX):
            for z in range(NZ):
                for k in range(NK):
                    pairs.append((linear(y, x, z, k), linear(*f(y, x, z, k))))
    return pairs


def to_plane(y, x, z, k):
    return (-z - y) % NY, x, y, k


def to_sibling(y, x, z, k):
    return y, x, z, 1 - k


def product_kernel(where, gathered, own, sib, m0, m1, m2, part_ref, diag_ref, g_v, r_v, m_v, acc, g_sem, r_sem, m_sem):
    core, plane = where[0], where[1]
    g_copies, r_copies = [], []
    for s in range(4):
        x = 2 * (core ^ (s // 2)) + s % 2
        block = (own, sib)[s // 2].at[:, pl.ds(s % 2 * ROWS, ROWS)]
        g_copies.append(pltpu.make_async_copy(gathered.at[:, x], g_v.at[s], g_sem.at[s]))
        r_copies.append(pltpu.make_async_copy(block, r_v.at[s], r_sem.at[s]))
        g_copies[s].start()
        r_copies[s].start()
    m_copies = [pltpu.make_async_copy(m, m_v.at[j], m_sem.at[j]) for j, m in enumerate((m0, m1, m2))]
    for copy in m_copies:
        copy.start()
    for s in range(4):
        g_copies[s].wait()
        r_copies[s].wait()
        product = lax.dot_general(g_v[s].reshape(NY * SL, ROWS), r_v[s], NT_DIMS, preferred_element_type=jnp.float32)
        if s == 0:
            acc[...] = product
        elif s < 3:
            acc[...] += product
        else:
            total = (acc[...] + product).astype(jnp.bfloat16).reshape(NY, SL, ROWS)
            for y in range(NY):
                part_ref[lax.rem(2 * NY - y - plane, NZ)] = total[y]
    for j in range(SUPERS):
        m_copies[j].wait()
        mine = part_ref[:, j * WL:(j + 1) * WL, :].reshape(NZ * WL, ROWS)
        diag = lax.dot_general(m_v[j].reshape(W, ROWS), mine, NT_DIMS, preferred_element_type=jnp.float32)
        diag_ref[:, j * NZ * WL:(j + 1) * NZ * WL] = diag.astype(jnp.bfloat16)


def products(where, *arrays):
    return pl.pallas_call(
        product_kernel,
        in_specs=[pl.BlockSpec(memory_space=pltpu.SMEM)] + [pl.BlockSpec(memory_space=pl.ANY)] * 6,
        out_specs=[pl.BlockSpec(memory_space=pltpu.VMEM)] * 2,
        scratch_shapes=[
            pltpu.VMEM((4, NY, SL, ROWS), jnp.bfloat16),
            pltpu.VMEM((4, ROWS, ROWS), jnp.bfloat16),
            pltpu.VMEM((SUPERS, NZ * NK, WL, ROWS), jnp.bfloat16),
            pltpu.VMEM((NY * SL, ROWS), jnp.float32),
            pltpu.SemaphoreType.DMA((4,)),
            pltpu.SemaphoreType.DMA((4,)),
            pltpu.SemaphoreType.DMA((SUPERS,)),
        ],
        out_shape=[
            jax.ShapeDtypeStruct((NZ, SL, ROWS), jnp.bfloat16),
            jax.ShapeDtypeStruct((W, SUPERS * NZ * WL), jnp.bfloat16),
        ],
        compiler_params=pltpu.CompilerParams(vmem_limit_bytes=56 * 1024 * 1024),
        cost_estimate=pl.CostEstimate(flops=4_800_000_000, bytes_accessed=14_000_000, transcendentals=0),
    )(where, *arrays)


def on_device(resident, factor, diag_inverse, anc_tiles, slot_tile):
    y, x, z, k = (lax.axis_index(a) for a in AXES)

    turned = factor.transpose(0, 2, 1)
    arrived = lax.ppermute(turned.reshape(SL, ROWS), AXES, permutation(to_plane))
    sib = lax.ppermute(resident, AXES, permutation(to_sibling))

    def mask_of(block):
        slots = lax.dynamic_slice(slot_tile, (block * SLOTS,), (SLOTS,))
        listed = jnp.any(anc_tiles[:, None, :] == slots[None, :, None], axis=2)
        return jnp.repeat(listed, TB, axis=1)[:, None, :]

    mask = mask_of(y * NX + x)
    masked = jnp.where(mask, turned, jnp.bfloat16(0))
    rows = [lax.all_gather(masked[j], COL, axis=0, tiled=False) for j in range(SUPERS)]

    moved = jnp.where(mask_of(z * NX + x), arrived.reshape(SUPERS, WL, ROWS), jnp.bfloat16(0)).reshape(SL, ROWS)
    near = lax.all_gather(moved, "x", axis=0, tiled=False)
    gathered = lax.all_gather(near, "y", axis=0, tiled=False)

    part, diag = products(jnp.stack([k, z]).astype(jnp.int32), gathered, resident, sib, *rows)

    summed = lax.psum_scatter(part.reshape(NZ * SL, ROWS), "z", scatter_dimension=0, tiled=True)
    summed = summed.reshape(SUPERS, WL, ROWS).astype(jnp.float32)
    new_cols = jnp.where(mask, -summed, 0.0).astype(jnp.bfloat16).transpose(0, 2, 1)

    spread = lax.all_to_all(diag.reshape(NY * NX, W // (NY * NX), SUPERS * NZ * WL), ROW, 0, 0, tiled=True)
    slab = jnp.sum(spread.astype(jnp.float32), axis=0).reshape(W // (NY * NX), SUPERS, NZ, WL)
    slab = slab.transpose(2, 0, 1, 3).reshape(NZ, W // (NY * NX), SL)
    slab = jnp.sum(lax.all_to_all(slab, "z", 0, 0, tiled=True), axis=0).astype(jnp.bfloat16)
    copies = jnp.broadcast_to(slab[None], (NY * NX,) + slab.shape)
    total = lax.all_to_all(copies, ROW, 0, 0, tiled=True)
    total = total.reshape(W, SUPERS, WL).transpose(1, 0, 2).astype(jnp.float32)
    return new_cols, diag_inverse + total


def solution(mesh):
    fine = Mesh(mesh.devices.reshape(NY, NX, NZ, NK), AXES)
    return jax.shard_map(
        on_device,
        mesh=fine,
        in_specs=(P(ROW, COL), P(None, ROW, COL), P(None, None, COL), P(), P()),
        out_specs=(P(None, ROW, COL), P(None, None, COL)),
        check_vma=False,
    )
```

```python
import jax
import jax.numpy as jnp
from jax import lax
from jax.experimental import pallas as pl
from jax.experimental.pallas import tpu as pltpu
from jax.sharding import Mesh, PartitionSpec as P

AXES = ("y", "x", "z", "k")
ROW, COL = ("y", "x"), ("z", "k")
NY, NX, NZ, NK = 8, 4, 8, 2
SUPERS = 3
W = 512
WL = 32
SL = SUPERS * WL
ROWS = 768
SLOTS = 3
CUT = 80
PIECES = ((0, 0, 32, 0, 0), (0, 32, 32, 1, 0), (0, 64, 16, 2, 0), (1, 0, 16, 2, 16))
TB = 256
NT_DIMS = (((1,), (1,)), ((), ()))


def linear(y, x, z, k):
    return ((y * NX + x) * NZ + z) * NK + k


def permutation(f):
    pairs = []
    for y in range(NY):
        for x in range(NX):
            for z in range(NZ):
                for k in range(NK):
                    pairs.append((linear(y, x, z, k), linear(*f(y, x, z, k))))
    return pairs


def to_plane(y, x, z, k):
    return (-z - y) % NY, x, y, k


def to_sibling(y, x, z, k):
    return y, x, z, 1 - k


def product_kernel(where, gathered, own, sib, m_most, m_few, s_most, s_few, part_ref, diag_ref,
                   g_v, r_v, m_v, acc, g_sem, r_sem, m_sem):
    core, plane = where[0], where[1]
    g_copies, r_copies, m_copies = [], [], []
    for s in range(4):
        x = 2 * (core ^ (s // 2)) + s % 2
        block = (own, sib)[s // 2].at[:, pl.ds(s % 2 * ROWS, ROWS)]
        g_copies.append(pltpu.make_async_copy(gathered.at[:, x], g_v.at[s], g_sem.at[s]))
        r_copies.append(pltpu.make_async_copy(block, r_v.at[s], r_sem.at[s]))
        g_copies[s].start()
        r_copies[s].start()
    for side, (many, rest) in enumerate(((m_most, m_few), (s_most, s_few))):
        for i, (src, first, rows, j, at) in enumerate(PIECES):
            m_copies.append(pltpu.make_async_copy(
                (many, rest)[src].at[:, pl.ds(first, rows), :],
                m_v.at[j, :, core ^ side, pl.ds(at, rows), :],
                m_sem.at[len(PIECES) * side + i],
            ))
            m_copies[-1].start()
    for s in range(4):
        g_copies[s].wait()
        r_copies[s].wait()
        product = lax.dot_general(g_v[s].reshape(NY * SL, ROWS), r_v[s], NT_DIMS, preferred_element_type=jnp.float32)
        if s == 0:
            acc[...] = product
        elif s < 3:
            acc[...] += product
        else:
            total = (acc[...] + product).astype(jnp.bfloat16).reshape(NY, SL, ROWS)
            for y in range(NY):
                part_ref[lax.rem(2 * NY - y - plane, NZ)] = total[y]
    for copy in m_copies:
        copy.wait()
    for j in range(SUPERS):
        mine = part_ref[:, j * WL:(j + 1) * WL, :].reshape(NZ * WL, ROWS)
        diag = lax.dot_general(m_v[j].reshape(W, ROWS), mine, NT_DIMS, preferred_element_type=jnp.float32)
        diag_ref[:, j * NZ * WL:(j + 1) * NZ * WL] = diag.astype(jnp.bfloat16)


def products(where, *arrays):
    return pl.pallas_call(
        product_kernel,
        in_specs=[pl.BlockSpec(memory_space=pltpu.SMEM)] + [pl.BlockSpec(memory_space=pl.ANY)] * 7,
        out_specs=[pl.BlockSpec(memory_space=pltpu.VMEM)] * 2,
        scratch_shapes=[
            pltpu.VMEM((4, NY, SL, ROWS), jnp.bfloat16),
            pltpu.VMEM((4, ROWS, ROWS), jnp.bfloat16),
            pltpu.VMEM((SUPERS, NZ, NK, WL, ROWS), jnp.bfloat16),
            pltpu.VMEM((NY * SL, ROWS), jnp.float32),
            pltpu.SemaphoreType.DMA((4,)),
            pltpu.SemaphoreType.DMA((4,)),
            pltpu.SemaphoreType.DMA((2 * len(PIECES),)),
        ],
        out_shape=[
            jax.ShapeDtypeStruct((NZ, SL, ROWS), jnp.bfloat16),
            jax.ShapeDtypeStruct((W, SUPERS * NZ * WL), jnp.bfloat16),
        ],
        compiler_params=pltpu.CompilerParams(vmem_limit_bytes=56 * 1024 * 1024),
        cost_estimate=pl.CostEstimate(flops=4_800_000_000, bytes_accessed=14_000_000, transcendentals=0),
    )(where, *arrays)


def on_device(resident, factor, diag_inverse, anc_tiles, slot_tile):
    y, x, z, k = (lax.axis_index(a) for a in AXES)

    turned = factor.transpose(0, 2, 1)
    arrived = lax.ppermute(turned.reshape(SL, ROWS), AXES, permutation(to_plane))
    sib = lax.ppermute(resident, AXES, permutation(to_sibling))

    def mask_of(block):
        slots = lax.dynamic_slice(slot_tile, (block * SLOTS,), (SLOTS,))
        listed = jnp.any(anc_tiles[:, None, :] == slots[None, :, None], axis=2)
        return jnp.repeat(listed, TB, axis=1)[:, None, :]

    mask = mask_of(y * NX + x)
    masked = jnp.where(mask, turned, jnp.bfloat16(0))
    flat = masked.reshape(SL, ROWS)

    def to_all(array, axis, size):
        return lax.all_to_all(jnp.broadcast_to(array[None], (size,) + array.shape), axis, 0, 0, tiled=True)

    m_few = to_all(flat[CUT:], "z", NZ)
    m_most = lax.all_gather(flat[:CUT], "z", axis=0, tiled=False)
    s_few = lax.ppermute(m_few, AXES, permutation(to_sibling))
    s_most = lax.ppermute(m_most, AXES, permutation(to_sibling))

    moved = jnp.where(mask_of(z * NX + x), arrived.reshape(SUPERS, WL, ROWS), jnp.bfloat16(0)).reshape(SL, ROWS)
    near = lax.all_gather(moved, "x", axis=0, tiled=False)
    gathered = lax.all_gather(near, "y", axis=0, tiled=False)

    part, diag = products(jnp.stack([k, z]).astype(jnp.int32), gathered, resident, sib, m_most, m_few, s_most, s_few)

    summed = lax.psum_scatter(part.reshape(NZ * SL, ROWS), "z", scatter_dimension=0, tiled=True)
    new_cols = jnp.where(mask, -summed.reshape(SUPERS, WL, ROWS), jnp.bfloat16(0)).transpose(0, 2, 1)

    spread = lax.all_to_all(diag.reshape(NY * NX, W // (NY * NX), SUPERS * NZ * WL), ROW, 0, 0, tiled=True)
    slab = jnp.sum(spread.astype(jnp.float32), axis=0).reshape(W // (NY * NX), SUPERS, NZ, WL)
    slab = slab.transpose(2, 0, 1, 3).reshape(NZ, W // (NY * NX), SL)
    slab = jnp.sum(lax.all_to_all(slab, "z", 0, 0, tiled=True), axis=0).astype(jnp.bfloat16)
    copies = jnp.broadcast_to(slab[None], (NY * NX,) + slab.shape)
    total = lax.all_to_all(copies, ROW, 0, 0, tiled=True)
    total = total.reshape(W, SL).T.reshape(SUPERS, WL, W).astype(jnp.float32)
    return new_cols, (diag_inverse.transpose(0, 2, 1) + total).transpose(0, 2, 1)


def solution(mesh):
    fine = Mesh(mesh.devices.reshape(NY, NX, NZ, NK), AXES)
    return jax.shard_map(
        on_device,
        mesh=fine,
        in_specs=(P(ROW, COL), P(None, ROW, COL), P(None, None, COL), P(), P()),
        out_specs=(P(None, ROW, COL), P(None, None, COL)),
        check_vma=False,
    )
```

```python
import jax
import jax.numpy as jnp
from jax import lax
from jax.experimental import pallas as pl
from jax.experimental.pallas import tpu as pltpu
from jax.sharding import Mesh, PartitionSpec as P

AXES = ("y", "x", "z", "k")
ROW, COL = ("y", "x"), ("z", "k")
NY, NX, NZ, NK = 8, 4, 8, 2
SUPERS = 3
W = 512
WL = 32
SL = SUPERS * WL
ROWS = 768
SLOTS = 3
CUT = 80
PIECES = ((0, 0, 32, 0, 0), (0, 32, 32, 1, 0), (0, 64, 16, 2, 0), (1, 0, 16, 2, 16))
TB = 256
NT_DIMS = (((1,), (1,)), ((), ()))


def linear(y, x, z, k):
    return ((y * NX + x) * NZ + z) * NK + k


def permutation(f):
    pairs = []
    for y in range(NY):
        for x in range(NX):
            for z in range(NZ):
                for k in range(NK):
                    pairs.append((linear(y, x, z, k), linear(*f(y, x, z, k))))
    return pairs


def to_plane(y, x, z, k):
    return (-z - y) % NY, x, y, k


def to_sibling(y, x, z, k):
    return y, x, z, 1 - k


def product_kernel(where, gathered, own, sib, m_most, m_few, s_most, s_few, part_ref, diag_ref,
                   g_v, r_v, m_v, acc, g_sem, r_sem, m_sem):
    core, plane = where[0], where[1]
    g_copies, r_copies, m_copies = [], [], []
    for s in range(4):
        x = 2 * (core ^ (s // 2)) + s % 2
        block = (own, sib)[s // 2].at[:, pl.ds(s % 2 * ROWS, ROWS)]
        g_copies.append(pltpu.make_async_copy(gathered.at[:, x], g_v.at[s], g_sem.at[s]))
        r_copies.append(pltpu.make_async_copy(block, r_v.at[s], r_sem.at[s]))
        g_copies[s].start()
        r_copies[s].start()
    for side, (many, rest) in enumerate(((m_most, m_few), (s_most, s_few))):
        for i, (src, first, rows, j, at) in enumerate(PIECES):
            m_copies.append(pltpu.make_async_copy(
                (many, rest)[src].at[:, pl.ds(first, rows), :],
                m_v.at[j, :, core ^ side, pl.ds(at, rows), :],
                m_sem.at[len(PIECES) * side + i],
            ))
            m_copies[-1].start()
    for s in range(4):
        g_copies[s].wait()
        r_copies[s].wait()
        product = lax.dot_general(g_v[s].reshape(NY * SL, ROWS), r_v[s], NT_DIMS, preferred_element_type=jnp.float32)
        if s == 0:
            acc[...] = product
        elif s < 3:
            acc[...] += product
        else:
            total = (acc[...] + product).astype(jnp.bfloat16).reshape(NY, SL, ROWS)
            for y in range(NY):
                part_ref[lax.rem(2 * NY - y - plane, NZ)] = total[y]
    for copy in m_copies:
        copy.wait()
    for j in range(SUPERS):
        mine = part_ref[:, j * WL:(j + 1) * WL, :].reshape(NZ * WL, ROWS)
        diag = lax.dot_general(m_v[j].reshape(W, ROWS), mine, NT_DIMS, preferred_element_type=jnp.float32)
        diag_ref[:, j * NZ * WL:(j + 1) * NZ * WL] = diag.astype(jnp.bfloat16)


def products(where, *arrays):
    return pl.pallas_call(
        product_kernel,
        in_specs=[pl.BlockSpec(memory_space=pltpu.SMEM)] + [pl.BlockSpec(memory_space=pl.ANY)] * 7,
        out_specs=[pl.BlockSpec(memory_space=pltpu.VMEM)] * 2,
        scratch_shapes=[
            pltpu.VMEM((4, NY, SL, ROWS), jnp.bfloat16),
            pltpu.VMEM((4, ROWS, ROWS), jnp.bfloat16),
            pltpu.VMEM((SUPERS, NZ, NK, WL, ROWS), jnp.bfloat16),
            pltpu.VMEM((NY * SL, ROWS), jnp.float32),
            pltpu.SemaphoreType.DMA((4,)),
            pltpu.SemaphoreType.DMA((4,)),
            pltpu.SemaphoreType.DMA((2 * len(PIECES),)),
        ],
        out_shape=[
            jax.ShapeDtypeStruct((NZ, SL, ROWS), jnp.bfloat16),
            jax.ShapeDtypeStruct((W, SUPERS * NZ * WL), jnp.bfloat16),
        ],
        compiler_params=pltpu.CompilerParams(vmem_limit_bytes=56 * 1024 * 1024),
        cost_estimate=pl.CostEstimate(flops=4_800_000_000, bytes_accessed=14_000_000, transcendentals=0),
    )(where, *arrays)


def on_device(resident, factor, diag_inverse, anc_tiles, slot_tile):
    y, x, z, k = (lax.axis_index(a) for a in AXES)

    turned = factor.transpose(0, 2, 1)
    arrived = lax.ppermute(turned.reshape(SL, ROWS), AXES, permutation(to_plane))
    sib = lax.ppermute(resident, AXES, permutation(to_sibling))

    def mask_of(block):
        slots = lax.dynamic_slice(slot_tile, (block * SLOTS,), (SLOTS,))
        listed = jnp.any(anc_tiles[:, None, :] == slots[None, :, None], axis=2)
        return jnp.repeat(listed, TB, axis=1)[:, None, :]

    mask = mask_of(y * NX + x)
    masked = jnp.where(mask, turned, jnp.bfloat16(0))
    flat = masked.reshape(SL, ROWS)

    def to_all(array, axis, size):
        return lax.all_to_all(jnp.broadcast_to(array[None], (size,) + array.shape), axis, 0, 0, tiled=True)

    m_few = to_all(flat[CUT:], "z", NZ)
    m_most = lax.all_gather(flat[:CUT], "z", axis=0, tiled=False)
    s_few = lax.ppermute(m_few, AXES, permutation(to_sibling))
    s_most = lax.ppermute(m_most, AXES, permutation(to_sibling))

    moved = jnp.where(mask_of(z * NX + x), arrived.reshape(SUPERS, WL, ROWS), jnp.bfloat16(0)).reshape(SL, ROWS)
    near = to_all(moved, "x", NX)
    gathered = lax.all_gather(near, "y", axis=0, tiled=False)

    part, diag = products(jnp.stack([k, z]).astype(jnp.int32), gathered, resident, sib, m_most, m_few, s_most, s_few)

    summed = lax.psum_scatter(part.reshape(NZ * SL, ROWS), "z", scatter_dimension=0, tiled=True)
    new_cols = jnp.where(mask, -summed.reshape(SUPERS, WL, ROWS), jnp.bfloat16(0)).transpose(0, 2, 1)

    spread = lax.all_to_all(diag.reshape(NY * NX, W // (NY * NX), SUPERS * NZ * WL), ROW, 0, 0, tiled=True)
    slab = jnp.sum(spread.astype(jnp.float32), axis=0).reshape(W // (NY * NX), SUPERS, NZ, WL)
    slab = slab.transpose(2, 0, 1, 3).reshape(NZ, W // (NY * NX), SL)
    slab = jnp.sum(lax.all_to_all(slab, "z", 0, 0, tiled=True), axis=0).astype(jnp.bfloat16)
    copies = jnp.broadcast_to(slab[None], (NY * NX,) + slab.shape)
    total = lax.all_to_all(copies, ROW, 0, 0, tiled=True)
    total = total.reshape(W, SL).T.reshape(SUPERS, WL, W).astype(jnp.float32)
    return new_cols, (diag_inverse.transpose(0, 2, 1) + total).transpose(0, 2, 1)


def solution(mesh):
    fine = Mesh(mesh.devices.reshape(NY, NX, NZ, NK), AXES)
    return jax.shard_map(
        on_device,
        mesh=fine,
        in_specs=(P(ROW, COL), P(None, ROW, COL), P(None, None, COL), P(), P()),
        out_specs=(P(None, ROW, COL), P(None, None, COL)),
        check_vma=False,
    )
```
